512 devices in a mesh: dp: 64 (over z, x, core), mp: 8 (over y).
Axes of the slice: x: 4, y: 8, z: 8, core: 2. Of those that a mesh axis runs over, the one named last changes fastest.
Arguments:
- grads: bfloat16 [64, 32, 512, 512], P('dp', None, 'mp'), may hold values from -0.5 to 0.5
- slot_blocks: int32 [64, 1], replicated, may hold values from 0 to 31, as said below
- counts: int32 [64], P('dp'), may hold values from 0 to 1, as said below
- left_stat: bfloat16 [64, 1, 512, 512], P('dp', None, 'mp'), may hold values from -6 to 6
- right_stat: bfloat16 [64, 1, 512, 512], P('dp', None, 'mp'), may hold values from -6 to 6
- left_root: bfloat16 [64, 1, 512, 512], P('dp', None, 'mp')
- right_root: bfloat16 [64, 1, 512, 512], P('dp', None, None, 'mp')
Outputs:
- left_new: bfloat16 [64, 1, 512, 512], P('dp', None, 'mp')
- right_new: bfloat16 [64, 1, 512, 512], P('dp', None, 'mp')
- update: bfloat16 [64, 1, 512, 512], P('dp', None, 'mp')
The draws below stay inside these ranges and needn't reach their ends.
Inputs may be any that keep to these rules, and one draw needn't show every extreme that they name: `slot_blocks`: every block 0 to 31 stands in exactly one live slot (s < counts[o]); ids in slots that are not live are arbitrary. `counts`: some owner has all 1 slots live.
All inputs are finite; a program needn't handle non-finite values.
Results may differ from the reference program's by a relative error of at most 0.0058.
Values may be sent and summed in bfloat16 or wider, within the bound.
No kernel may reach another device: no remote copies, remote signals or barrier semaphores. Data moves between devices by JAX's collectives and lax.ppermute only.
A program may use at most 64 MiB of HBM per device.

```python
import jax
import jax.numpy as jnp
from jax import lax

BLOCK = 512
MAXB = 1
NBLK = 32
N_DP = 64


def assign_slots(key):
    owners = jax.random.permutation(jax.random.fold_in(key, 11), N_DP).astype(jnp.int32)
    blocks = jnp.arange(NBLK, dtype=jnp.int32)
    owner_of = owners[blocks // MAXB]
    slot_of = blocks % MAXB
    filler = jax.random.randint(jax.random.fold_in(key, 12), (N_DP, MAXB), 0, NBLK, dtype=jnp.int32)
    listing = filler.at[owner_of, slot_of].set(blocks)
    totals = jnp.zeros((N_DP,), jnp.int32).at[owner_of].add(1)
    return (listing, totals)


def draw_slot_blocks(key, part):
    listing, totals = assign_slots(key)
    return listing


def draw_counts(key, part):
    listing, totals = assign_slots(key)
    return totals


def root_from(diag_key, noise):
    shape = (N_DP, MAXB, BLOCK, BLOCK)
    diag = jnp.exp(jax.random.uniform(diag_key, shape, jnp.float32, -0.7, 0.7))
    rows = lax.broadcasted_iota(jnp.int32, shape, 2)
    cols = lax.broadcasted_iota(jnp.int32, shape, 3)
    return jnp.where(rows == cols, diag, noise * (0.5 / math_sqrt(BLOCK))).astype(jnp.bfloat16)


def math_sqrt(value):
    return float(value) ** 0.5


def draw_left_root(key, part):
    key = jax.random.fold_in(key, 3)
    shape = (N_DP, MAXB, BLOCK, BLOCK)
    noise = jax.random.normal(jax.random.fold_in(key, 1), shape, jnp.float32)
    return root_from(jax.random.fold_in(key, 2), noise)


def draw_right_root(key, part):
    key = jax.random.fold_in(key, 4)
    shape = (N_DP, MAXB, BLOCK, BLOCK)
    noise = jax.random.normal(jax.random.fold_in(key, 1), shape, jnp.float32)
    return root_from(jax.random.fold_in(key, 2), noise)


def level_of(rng, dims, shards, low, top_value):
    def one(axis_at, shards_of):
        steps = jax.random.uniform(jax.random.fold_in(jax.random.fold_in(rng, 6), axis_at), (shards_of,), jnp.float32, low / len(shards), top_value / len(shards))
        return jnp.repeat(jnp.exp(steps), dims[axis_at] // shards_of).reshape((-1,) + (1,) * (len(dims) - axis_at - 1))

    factor_of = one(*shards[0])
    for cut in shards[1:]:
        factor_of = factor_of * one(*cut)
    return factor_of


def scatter_about(key, extent, spread, reach, cuts=(), kind=jnp.bfloat16):
    drawn = jax.random.normal(key, extent, jnp.float32) * spread
    if len(cuts) > 0:
        drawn = level_of(key, extent, cuts, -0.22, 0.18) * drawn
    return jnp.clip(drawn, min=-reach, max=reach).astype(kind)


def setup_inputs(seed: int = 0) -> dict:
    arg_keys = jax.random.split(jax.random.key(seed), 8)
    return {
        "grads": scatter_about(arg_keys[0], (N_DP, NBLK, BLOCK, BLOCK), 0.03125, 0.5, ((0, 64), (2, 8))),
        "slot_blocks": draw_slot_blocks(jax.random.fold_in(arg_keys[7], 71), 0),
        "counts": draw_counts(jax.random.fold_in(arg_keys[7], 71), 0),
        "left_stat": scatter_about(arg_keys[3], (N_DP, MAXB, BLOCK, BLOCK), 1.0, 6.0, ((0, 64), (2, 8))),
        "right_stat": scatter_about(arg_keys[4], (N_DP, MAXB, BLOCK, BLOCK), 1.0, 6.0, ((0, 64), (2, 8))),
        "left_root": draw_left_root(jax.random.fold_in(arg_keys[7], 71), 0),
        "right_root": draw_right_root(jax.random.fold_in(arg_keys[7], 71), 0),
    }


BETA = 0.9
RATE = 0.5
EPS = 1e-06

def slot_update(total_block, lstat, rstat, lroot, rroot):
    g = total_block.astype(jnp.bfloat16)
    gram_left = jnp.dot(g, g.T, preferred_element_type=jnp.float32)
    gram_right = jnp.dot(g.T, g, preferred_element_type=jnp.float32)
    new_left = (BETA * lstat.astype(jnp.float32) + (1.0 - BETA) * gram_left).astype(jnp.bfloat16)
    new_right = (BETA * rstat.astype(jnp.float32) + (1.0 - BETA) * gram_right).astype(jnp.bfloat16)
    middle = jnp.dot(g, rroot, preferred_element_type=jnp.float32).astype(jnp.bfloat16)
    pre = jnp.dot(lroot, middle, preferred_element_type=jnp.float32)
    g_float = g.astype(jnp.float32)
    scale = jnp.sqrt(jnp.mean(g_float * g_float)) / jnp.sqrt(jnp.mean(pre * pre) + EPS)
    new_update = (-RATE * scale * pre).astype(jnp.bfloat16)
    return (new_left, new_right, new_update)

def reference(grads, slot_blocks, counts, left_stat, right_stat, left_root, right_root):
    total = lax.optimization_barrier(jnp.sum(grads.astype(jnp.float32), axis=0))
    flat_shape = (N_DP * MAXB, BLOCK, BLOCK)
    lflat = left_stat.reshape(flat_shape)
    rflat = right_stat.reshape(flat_shape)
    lroots = left_root.reshape(flat_shape)
    rroots = right_root.reshape(flat_shape)
    live = jnp.arange(MAXB, dtype=jnp.int32)[None, :] < counts[:, None]
    out_left, out_right = (lflat, rflat)
    out_update = jnp.zeros(flat_shape, jnp.bfloat16)
    for block in range(NBLK):
        match = (live & (slot_blocks == block)).astype(jnp.int32).reshape(-1)
        where = jnp.argmax(match).astype(jnp.int32)
        new_left, new_right, new_update = slot_update(total[block], lflat[where], rflat[where], lroots[where], rroots[where])
        out_left = out_left.at[where].set(new_left)
        out_right = out_right.at[where].set(new_right)
        out_update = out_update.at[where].set(new_update)
    full_shape = (N_DP, MAXB, BLOCK, BLOCK)
    return (out_left.reshape(full_shape), out_right.reshape(full_shape), out_update.reshape(full_shape))
```

```python
import functools

import jax
import jax.numpy as jnp
from jax import lax
from jax.experimental import pallas as pl
from jax.experimental.pallas import tpu as pltpu
from jax.sharding import Mesh
from jax.sharding import PartitionSpec as P

BETA = 0.9
RATE = 0.5
EPS = 1e-06
NZ, NX, NC = 8, 4, 2
F32 = jnp.float32
BF16 = jnp.bfloat16
DP = ("z", "x", "c")


def route_kernel(ids_ref, terms_ref, out_ref, held_ref):
    nblk = held_ref.shape[0]
    total = terms_ref[0].astype(F32)
    for i in range(1, NX):
        total += terms_ref[i].astype(F32)
    held_ref[...] = total.astype(BF16)

    def body(i, carry):
        for k in range(8):
            o = i * 8 + k
            b = jnp.clip(ids_ref[o], 0, nblk - 1)
            out_ref[o] = held_ref[b]
        return carry

    lax.fori_loop(0, out_ref.shape[0] // 8, body, 0)


def collect_kernel(terms_ref, out_ref):
    n_out, rows = out_ref.shape[0], terms_ref.shape[1]
    for x in range(NX):
        for c in range(NC):
            total = terms_ref[x * NC + c].astype(F32)
            for z in range(1, NZ):
                total += terms_ref[(z * NX + x) * NC + c].astype(F32)
            low = total.astype(BF16)
            for k in range(n_out):
                out_ref[k, pl.ds(c * rows, rows), pl.ds(x * 128, 128)] = low


def finish_kernel(live_ref, g_ref, lstat_ref, rstat_ref, roots_ref, left_ref, right_ref, update_ref, gram_ref, pre_ref):
    n_mp, _, rows, width = roots_ref.shape
    m = live_ref[1]
    alive = live_ref[0] > 0
    mine = pl.ds(pl.multiple_of(m * rows, rows), rows)
    g = g_ref[...]
    cells = float(width * width)
    nt = (((1,), (1,)), ((), ()))
    tn = (((0,), (0,)), ((), ()))
    gram_left = lax.dot_general(g_ref[mine, :], g, nt, preferred_element_type=F32)
    lstat, rstat = lstat_ref[...], rstat_ref[...]
    new_left = (BETA * lstat.astype(F32) + (1.0 - BETA) * gram_left).astype(BF16)
    left_ref[...] = jnp.where(alive, new_left, lstat)
    gram_ref[...] = lax.dot_general(g, g, tn, preferred_element_type=F32)
    new_right = (BETA * rstat.astype(F32) + (1.0 - BETA) * gram_ref[mine, :]).astype(BF16)
    right_ref[...] = jnp.where(alive, new_right, rstat)
    lroot = roots_ref[:, 0].reshape(width, width)
    rroot_t = roots_ref[:, 1].reshape(width, width)
    middle = lax.dot_general(g, rroot_t, nt, preferred_element_type=F32).astype(BF16)
    pre = jnp.dot(lroot, middle, preferred_element_type=F32)
    pre_ref[...] = pre
    g_float = g.astype(F32)
    squares = jnp.sum(g_float * g_float)
    pre_squares = jnp.sum(pre * pre)
    top = jnp.full((1, 1), squares, F32) / cells
    bottom = jnp.full((1, 1), pre_squares, F32) / cells + EPS
    scale = jnp.sqrt(top) / jnp.sqrt(bottom)
    new_update = (-RATE * scale * pre_ref[mine, :]).astype(BF16)
    update_ref[...] = jnp.where(alive, new_update, jnp.zeros_like(new_update))


def on_device(grads, slot_blocks, counts, left_stat, right_stat, left_root, right_root):
    terms = grads[0]
    nblk, rows, width = terms.shape
    half, quarter = rows // NC, width // NX
    vmem = pl.BlockSpec(memory_space=pltpu.VMEM)
    smem = pl.BlockSpec(memory_space=pltpu.SMEM)
    limit = pltpu.CompilerParams(vmem_limit_bytes=48 * 1024 * 1024)
    n_mp = width // rows

    roots = jnp.stack([left_root[0, 0], right_root[0, 0].T])
    roots_all = lax.all_gather(roots, "mp", axis=0)

    core = lax.axis_index("c")
    halves = terms.reshape(nblk, NC, half, width)
    away = lax.dynamic_index_in_dim(halves, 1 - core, 1, keepdims=False)
    here = lax.dynamic_index_in_dim(halves, core, 1, keepdims=False)
    come = lax.ppermute(away, "c", [(0, 1), (1, 0)])
    pair = (here.astype(F32) + come.astype(F32)).astype(BF16)
    pair = pair.reshape(nblk, half, NX, quarter).transpose(2, 0, 1, 3)
    along_x = lax.all_to_all(pair, "x", 0, 0, tiled=True)

    owners = slot_blocks.shape[0]
    routed = pl.pallas_call(
        route_kernel,
        out_shape=jax.ShapeDtypeStruct((owners, half, quarter), BF16),
        in_specs=[smem, vmem],
        out_specs=vmem,
        scratch_shapes=[pltpu.VMEM((nblk, half, quarter), BF16)],
        compiler_params=limit,
    )(slot_blocks[:, 0], along_x)
    owned = lax.all_to_all(routed, DP, 0, 0, tiled=True)
    copies = pl.pallas_call(
        collect_kernel,
        out_shape=jax.ShapeDtypeStruct((n_mp, rows, width), BF16),
        in_specs=[vmem],
        out_specs=vmem,
        compiler_params=limit,
    )(owned)
    g = lax.all_to_all(copies, "mp", 0, 0, tiled=True).reshape(width, width)

    live = jnp.stack([counts[0], lax.axis_index("mp").astype(jnp.int32)])
    shape = jax.ShapeDtypeStruct((rows, width), BF16)
    outs = pl.pallas_call(
        finish_kernel,
        out_shape=(shape, shape, shape),
        in_specs=[smem, vmem, vmem, vmem, vmem],
        out_specs=(vmem, vmem, vmem),
        scratch_shapes=[pltpu.VMEM((width, width), F32), pltpu.VMEM((width, width), F32)],
        compiler_params=limit,
    )(live, g, left_stat[0, 0], right_stat[0, 0], roots_all)
    return tuple(o[None, None] for o in outs)


def solution(mesh):
    fine = Mesh(mesh.devices.reshape(NZ, NX, NC, mesh.devices.shape[1]), ("z", "x", "c", "mp"))
    rows = P(DP, None, "mp", None)
    return jax.shard_map(
        on_device,
        mesh=fine,
        in_specs=(rows, P(), P(DP), rows, rows, rows, P(DP, None, None, "mp")),
        out_specs=(rows, rows, rows),
        check_vma=False,
    )
```

```python
import jax
import jax.numpy as jnp
from jax import lax
from jax.experimental import pallas as pl
from jax.experimental.pallas import tpu as pltpu
from jax.sharding import Mesh
from jax.sharding import PartitionSpec as P

BETA = 0.9
RATE = 0.5
EPS = 1e-06
NZ, NX, NC = 8, 4, 2
F32 = jnp.float32
BF16 = jnp.bfloat16
BATCH = 8
DP = ("z", "x", "c")
BACK = (0, 1, 7, 2, 6, 3, 5, 4)


def pair_kernel(core_ref, terms_ref, come_ref, out_ref):
    total = (terms_ref[:, 0].astype(F32) + come_ref[...].astype(F32)).astype(BF16)
    for x in range(NX):
        out_ref[x] = total[:, :, x * 128 : (x + 1) * 128]


def route_kernel(ids_ref, terms_ref, out_ref, held_ref):
    nblk = held_ref.shape[0]
    total = terms_ref[0].astype(F32)
    for x in range(1, NX):
        total += terms_ref[x].astype(F32)
    held_ref[...] = total.astype(BF16)

    def body(i, carry):
        for k in range(8):
            o = i * 8 + k
            b = jnp.clip(ids_ref[o], 0, nblk - 1)
            out_ref[o] = held_ref[b]
        return carry

    lax.fori_loop(0, out_ref.shape[0] // 8, body, 0)


def collect_kernel(terms_ref, out_ref):
    n_out, rows = out_ref.shape[0], terms_ref.shape[1]
    for x in range(NX):
        for c in range(NC):
            total = terms_ref[x * NC + c].astype(F32)
            for z in range(1, NZ):
                total += terms_ref[(z * NX + x) * NC + c].astype(F32)
            low = total.astype(BF16)
            for k in range(n_out):
                out_ref[k, pl.ds(c * rows, rows), pl.ds(x * 128, 128)] = low


def finish_kernel(live_ref, parts_ref, lstat_ref, rstat_ref, *refs):
    n_mp, rows, width = parts_ref.shape
    root_refs, refs = refs[:n_mp], refs[n_mp:]
    left_ref, right_ref, update_ref, g_ref, gram_ref, lroot_ref, rroot_ref = refs
    m = live_ref[1]
    alive = live_ref[0] > 0
    mine = pl.ds(pl.multiple_of(m * rows, rows), rows)
    for k in range(n_mp):
        g_ref[pl.ds(k * rows, rows), :] = parts_ref[k]
    g = g_ref[...]
    cells = float(width * width)
    nt = (((1,), (1,)), ((), ()))
    tn = (((0,), (0,)), ((), ()))
    gram_left = lax.dot_general(g_ref[mine, :], g, nt, preferred_element_type=F32)
    lstat, rstat = lstat_ref[...], rstat_ref[...]
    new_left = (BETA * lstat.astype(F32) + (1.0 - BETA) * gram_left).astype(BF16)
    left_ref[...] = jnp.where(alive, new_left, lstat)
    gram_ref[...] = lax.dot_general(g, g, tn, preferred_element_type=F32)
    new_right = (BETA * rstat.astype(F32) + (1.0 - BETA) * gram_ref[mine, :]).astype(BF16)
    right_ref[...] = jnp.where(alive, new_right, rstat)
    for i, (ref, back) in enumerate(zip(root_refs, BACK)):
        lroot_ref[pl.ds(i * rows, rows), :] = ref[0]
        place = lax.rem(m + n_mp - back, n_mp) * rows
        rroot_ref[pl.ds(pl.multiple_of(place, rows), rows), :] = ref[1]
    middle = lax.dot_general(g, rroot_ref[...], nt, preferred_element_type=F32).astype(BF16)
    pre = jnp.dot(lroot_ref[...], middle, preferred_element_type=F32)
    g_float = g.astype(F32)
    squares = jnp.sum(g_float * g_float)
    pre_squares = jnp.sum(pre * pre)
    top = jnp.full((1, 1), squares, F32) / cells
    bottom = jnp.full((1, 1), pre_squares, F32) / cells + EPS
    scale = jnp.sqrt(top) / jnp.sqrt(bottom)
    new_update = (-RATE * scale * pre[:rows]).astype(BF16)
    update_ref[...] = jnp.where(alive, new_update, jnp.zeros_like(new_update))


VMEM = pl.BlockSpec(memory_space=pltpu.VMEM)
SMEM = pl.BlockSpec(memory_space=pltpu.SMEM)
LIMIT = pltpu.CompilerParams(vmem_limit_bytes=16 * 1024 * 1024)


def kernel_call(kernel, out_shape, scratch, scalars, *arrays):
    return pl.pallas_call(
        kernel,
        out_shape=out_shape,
        in_specs=[SMEM] * len(scalars) + [VMEM] * len(arrays),
        out_specs=jax.tree.map(lambda _: VMEM, out_shape),
        scratch_shapes=scratch,
        compiler_params=LIMIT,
    )(*scalars, *arrays)


def bf16(*shape):
    return jax.ShapeDtypeStruct(shape, BF16)


def on_device(grads, slot_blocks, counts, left_stat, right_stat, left_root, right_root):
    terms = grads[0]
    nblk, rows, width = terms.shape
    n_mp = width // rows
    core = lax.axis_index("c")

    half, quarter = rows // NC, width // NX
    halves = terms.reshape(nblk, NC, half, width)
    away = lax.dynamic_index_in_dim(halves, 1 - core, 1, keepdims=False)
    come = lax.ppermute(away, "c", [(0, 1), (1, 0)])

    def shift(a, k):
        return lax.ppermute(a, "mp", [(i, (i + k) % n_mp) for i in range(n_mp)])

    own = jnp.stack([left_root[0, 0], right_root[0, 0].T])
    pairs = pl.pallas_call(
        pair_kernel,
        grid_spec=pltpu.PrefetchScalarGridSpec(
            num_scalar_prefetch=1,
            grid=(nblk // BATCH,),
            in_specs=[
                pl.BlockSpec((BATCH, 1, half, width), lambda i, core: (i, core[0], 0, 0)),
                pl.BlockSpec((BATCH, half, width), lambda i, core: (i, 0, 0)),
            ],
            out_specs=pl.BlockSpec((NX, BATCH, half, quarter), lambda i, core: (0, i, 0, 0)),
        ),
        out_shape=bf16(NX, nblk, half, quarter),
        compiler_params=LIMIT,
    )(core.astype(jnp.int32)[None], halves, come)
    along_x = lax.all_to_all(pairs, "x", 0, 0, tiled=True)
    one = (shift(own, 1), shift(own, -1))
    along_x, one = lax.optimization_barrier((along_x, one))
    routed = kernel_call(
        route_kernel,
        bf16(slot_blocks.shape[0], half, quarter),
        [pltpu.VMEM((nblk, half, quarter), BF16)],
        (slot_blocks[:, 0],),
        along_x,
    )
    live = jnp.stack([counts[0], lax.axis_index("mp").astype(jnp.int32)])
    routed, live = lax.optimization_barrier((routed, live))
    owned = lax.all_to_all(routed, DP, 0, 0, tiled=True)
    two = (shift(one[0], 1), shift(one[1], -1))
    three = (shift(two[0], 1), shift(two[1], -1))
    owned, three = lax.optimization_barrier((owned, three))
    copies = kernel_call(collect_kernel, bf16(n_mp, rows, width), [], (), owned)
    g = lax.all_to_all(copies, "mp", 0, 0, tiled=True)
    four = shift(three[0], 1)
    roots = (own, *one, *two, *three, four)
    shape = bf16(rows, width)
    outs = kernel_call(
        finish_kernel,
        (shape, shape, shape),
        [pltpu.VMEM((width, width), BF16), pltpu.VMEM((width, width), F32)] + [pltpu.VMEM((width, width), BF16)] * 2,
        (live,),
        g,
        left_stat[0, 0],
        right_stat[0, 0],
        *roots,
    )
    return tuple(o[None, None] for o in outs)


def solution(mesh):
    fine = Mesh(mesh.devices.reshape(NZ, NX, NC, mesh.devices.shape[1]), ("z", "x", "c", "mp"))
    rows = P(DP, None, "mp", None)
    return jax.shard_map(
        on_device,
        mesh=fine,
        in_specs=(rows, P(), P(DP), rows, rows, rows, P(DP, None, None, "mp")),
        out_specs=(rows, rows, rows),
        check_vma=False,
    )
```

```python
import jax
import jax.numpy as jnp
from jax import lax
from jax.experimental import pallas as pl
from jax.experimental.pallas import tpu as pltpu
from jax.sharding import Mesh
from jax.sharding import PartitionSpec as P

BETA = 0.9
RATE = 0.5
EPS = 1e-06
NH, NL, NX, NC = 4, 2, 4, 2
F32 = jnp.float32
BF16 = jnp.bfloat16
BATCH = 16
SLOTS = 32
DP = ("zh", "zl", "x", "c")
BACK = ((0,), (4,), (1,), (7,), (5, 2), (3, 6))


def away_kernel(core_ref, terms_ref, out_ref, sem):
    copy = pltpu.make_async_copy(terms_ref.at[:, 1 - core_ref[0]], out_ref, sem)
    copy.start()
    copy.wait()


def pair_kernel(core_ref, terms_ref, come_ref, out_ref):
    batch = pl.ds(pl.program_id(0) * BATCH, BATCH)
    total = (terms_ref[batch, core_ref[0]].astype(F32) + come_ref[batch].astype(F32)).astype(BF16)
    rows = out_ref.shape[2]
    for z in range(NL):
        for x in range(NX):
            out_ref[z * NX + x] = total[:, z * rows : (z + 1) * rows, x * 128 : (x + 1) * 128]


def route_kernel(ids_ref, terms_ref, out_ref, held_ref):
    nblk = held_ref.shape[0]
    first = pl.program_id(0) * out_ref.shape[0]

    @pl.when(first == 0)
    def _():
        total = terms_ref[0].astype(F32)
        for i in range(1, NL * NX):
            total += terms_ref[i].astype(F32)
        held_ref[...] = total.astype(BF16)

    for k in range(out_ref.shape[0]):
        b = jnp.clip(ids_ref[first + k], 0, nblk - 1)
        out_ref[k] = held_ref[b]


def collect_kernel(terms_ref, out_ref):
    n_out, rows = out_ref.shape[0], terms_ref.shape[1]
    parts = NL * NX * NC
    for z in range(NL):
        for x in range(NX):
            for c in range(NC):
                part = (z * NX + x) * NC + c
                total = terms_ref[part].astype(F32)
                for h in range(1, NH):
                    total += terms_ref[h * parts + part].astype(F32)
                low = total.astype(BF16)
                for k in range(n_out):
                    out_ref[k, pl.ds((c * NL + z) * rows, rows), pl.ds(x * 128, 128)] = low


def finish_kernel(live_ref, parts_ref, lstat_ref, rstat_ref, *refs):
    n_mp, rows, width = parts_ref.shape
    root_refs, refs = refs[: len(BACK)], refs[len(BACK) :]
    left_ref, right_ref, update_ref, gram_ref, lroot_ref, rroot_ref = refs
    m = live_ref[1]
    alive = live_ref[0] > 0
    g = parts_ref[...].reshape(width, width)
    cells = float(width * width)
    nt = (((1,), (1,)), ((), ()))
    tn = (((0,), (0,)), ((), ()))
    gram_left = lax.dot_general(parts_ref[m], g, nt, preferred_element_type=F32)
    lstat, rstat = lstat_ref[...], rstat_ref[...]
    new_left = (BETA * lstat.astype(F32) + (1.0 - BETA) * gram_left).astype(BF16)
    left_ref[...] = jnp.where(alive, new_left, lstat)
    cols = parts_ref[:, :, pl.ds(pl.multiple_of(lax.div(m, 2) * 128, 128), 128)].reshape(width, 128)
    gram_ref[...] = lax.dot_general(cols, g, tn, preferred_element_type=F32)
    gram_right = gram_ref[pl.ds(pl.multiple_of(lax.rem(m, 2) * rows, rows), rows), :]
    new_right = (BETA * rstat.astype(F32) + (1.0 - BETA) * gram_right).astype(BF16)
    right_ref[...] = jnp.where(alive, new_right, rstat)
    blocks = [(ref.at[k], back) for ref, backs in zip(root_refs, BACK) for k, back in enumerate(backs)]
    for i, (ref, back) in enumerate(blocks):
        lroot_ref[pl.ds(i * rows, rows), :] = ref[0]
        place = lax.rem(m + n_mp - back, n_mp) * rows
        rroot_ref[pl.ds(pl.multiple_of(place, rows), rows), :] = ref[1]
    middle = lax.dot_general(g, rroot_ref[...], nt, preferred_element_type=F32).astype(BF16)
    pre = jnp.dot(lroot_ref[...], middle, preferred_element_type=F32)
    g_float = g.astype(F32)
    squares = jnp.sum(g_float * g_float)
    pre_squares = jnp.sum(pre * pre)
    top = jnp.full((1, 1), squares, F32) / cells
    bottom = jnp.full((1, 1), pre_squares, F32) / cells + EPS
    scale = jnp.sqrt(top) / jnp.sqrt(bottom)
    new_update = (-RATE * scale * pre[:rows]).astype(BF16)
    update_ref[...] = jnp.where(alive, new_update, jnp.zeros_like(new_update))


VMEM = pl.BlockSpec(memory_space=pltpu.VMEM)
SMEM = pl.BlockSpec(memory_space=pltpu.SMEM)
LIMIT = pltpu.CompilerParams(vmem_limit_bytes=16 * 1024 * 1024)


def kernel_call(kernel, out_shape, scratch, scalars, *arrays):
    return pl.pallas_call(
        kernel,
        out_shape=out_shape,
        in_specs=[SMEM] * len(scalars) + [VMEM] * len(arrays),
        out_specs=jax.tree.map(lambda _: VMEM, out_shape),
        scratch_shapes=scratch,
        compiler_params=LIMIT,
    )(*scalars, *arrays)


def bf16(*shape):
    return jax.ShapeDtypeStruct(shape, BF16)


def on_device(grads, slot_blocks, counts, left_stat, right_stat, left_root, right_root):
    terms = grads[0]
    nblk, rows, width = terms.shape
    n_mp = width // rows
    core = lax.axis_index("c")

    half, piece, quarter = rows // NC, rows // (NC * NL), width // NX
    halves = terms.reshape(nblk, NC, half, width)
    away = pl.pallas_call(
        away_kernel,
        out_shape=bf16(nblk, half, width),
        in_specs=[SMEM, pl.BlockSpec(memory_space=pltpu.HBM)],
        out_specs=VMEM,
        scratch_shapes=[pltpu.SemaphoreType.DMA],
        compiler_params=LIMIT,
    )(core.astype(jnp.int32)[None], halves)
    come = lax.ppermute(away, "c", [(0, 1), (1, 0)])

    def shift(a, k):
        return lax.ppermute(a, "mp", [(i, (i + k) % n_mp) for i in range(n_mp)])

    own = jnp.stack([left_root[0, 0], right_root[0, 0].T])[None]
    pairs = pl.pallas_call(
        pair_kernel,
        grid=(nblk // BATCH,),
        out_shape=bf16(NL * NX, nblk, piece, quarter),
        in_specs=[SMEM, VMEM, VMEM],
        out_specs=pl.BlockSpec((NL * NX, BATCH, piece, quarter), lambda i: (0, i, 0, 0)),
        compiler_params=LIMIT,
    )(core.astype(jnp.int32)[None], halves, come)
    along_x = lax.all_to_all(pairs, ("zl", "x"), 0, 0, tiled=True)
    four, one, seven = shift(own, 4), shift(own, 1), shift(own, -1)
    along_x, four, one, seven = lax.optimization_barrier((along_x, four, one, seven))
    owners = slot_blocks.shape[0]
    routed = pl.pallas_call(
        route_kernel,
        grid=(owners // SLOTS,),
        out_shape=bf16(owners, piece, quarter),
        in_specs=[SMEM, VMEM],
        out_specs=pl.BlockSpec((SLOTS, piece, quarter), lambda i: (i, 0, 0)),
        scratch_shapes=[pltpu.VMEM((nblk, piece, quarter), BF16)],
        compiler_params=LIMIT,
    )(slot_blocks[:, 0], along_x)
    live = jnp.stack([counts[0], lax.axis_index("mp").astype(jnp.int32)])
    routed, live = lax.optimization_barrier((routed, live))
    owned = lax.all_to_all(routed, DP, 0, 0, tiled=True)
    up = shift(jnp.concatenate([four, one]), 1)
    down = shift(jnp.concatenate([four, seven]), -1)
    owned, up, down = lax.optimization_barrier((owned, up, down))
    copies = kernel_call(collect_kernel, bf16(n_mp, rows, width), [], (), owned)
    g = lax.all_to_all(copies, "mp", 0, 0, tiled=True)
    roots = (own, four, one, seven, up, down)
    shape = bf16(rows, width)
    outs = kernel_call(
        finish_kernel,
        (shape, shape, shape),
        [pltpu.VMEM((128, width), F32)] + [pltpu.VMEM((width, width), BF16)] * 2,
        (live,),
        g,
        left_stat[0, 0],
        right_stat[0, 0],
        *roots,
    )
    return tuple(o[None, None] for o in outs)


def solution(mesh):
    fine = Mesh(mesh.devices.reshape(NH, NL, NX, NC, mesh.devices.shape[1]), (*DP, "mp"))
    rows = P(DP, None, "mp", None)
    return jax.shard_map(
        on_device,
        mesh=fine,
        in_specs=(rows, P(), P(DP), rows, rows, rows, P(DP, None, None, "mp")),
        out_specs=(rows, rows, rows),
        check_vma=False,
    )
```

```python
import jax
import jax.numpy as jnp
from jax import lax
from jax.experimental import pallas as pl
from jax.experimental.pallas import tpu as pltpu
from jax.sharding import Mesh
from jax.sharding import PartitionSpec as P

BETA = 0.9
RATE = 0.5
EPS = 1e-06
NH, NL, NX, NC = 4, 2, 4, 2
F32 = jnp.float32
BF16 = jnp.bfloat16
BATCH = 32
SLOTS = 64
DP = ("zh", "zl", "x", "c")
BACK = ((0,), (4,), (1,), (7,), (5, 2), (3, 6))


def away_kernel(core_ref, terms_ref, out_ref, sem):
    copy = pltpu.make_async_copy(terms_ref.at[:, 1 - core_ref[0]], out_ref, sem)
    copy.start()
    copy.wait()


def pair_kernel(core_ref, terms_ref, come_ref, out_ref):
    batch = pl.ds(pl.program_id(0) * BATCH, BATCH)
    total = (terms_ref[batch, core_ref[0]].astype(F32) + come_ref[batch].astype(F32)).astype(BF16)
    rows = out_ref.shape[2]
    for z in range(NL):
        for x in range(NX):
            out_ref[z * NX + x] = total[:, z * rows : (z + 1) * rows, x * 128 : (x + 1) * 128]


def route_kernel(ids_ref, terms_ref, out_ref, held_ref):
    nblk = held_ref.shape[0]
    first = pl.program_id(0) * out_ref.shape[0]

    @pl.when(first == 0)
    def _():
        total = terms_ref[0].astype(F32)
        for i in range(1, NL * NX):
            total += terms_ref[i].astype(F32)
        held_ref[...] = total.astype(BF16)

    for k in range(out_ref.shape[0]):
        b = jnp.clip(ids_ref[first + k], 0, nblk - 1)
        out_ref[k] = held_ref[b]


def collect_kernel(terms_ref, out_ref):
    n_out, rows = out_ref.shape[0], terms_ref.shape[1]
    parts = NL * NX * NC
    for z in range(NL):
        for x in range(NX):
            for c in range(NC):
                part = (z * NX + x) * NC + c
                total = terms_ref[part].astype(F32)
                for h in range(1, NH):
                    total += terms_ref[h * parts + part].astype(F32)
                low = total.astype(BF16)
                for k in range(n_out):
                    out_ref[k, pl.ds((c * NL + z) * rows, rows), pl.ds(x * 128, 128)] = low


def finish_kernel(live_ref, parts_ref, lstat_ref, rstat_ref, *refs):
    n_mp, rows, width = parts_ref.shape
    root_refs, refs = refs[: len(BACK)], refs[len(BACK) :]
    left_ref, right_ref, update_ref, gram_ref, lroot_ref, rroot_ref = refs
    m = live_ref[1]
    alive = live_ref[0] > 0
    g = parts_ref[...].reshape(width, width)
    cells = float(width * width)
    nt = (((1,), (1,)), ((), ()))
    tn = (((0,), (0,)), ((), ()))
    gram_left = lax.dot_general(parts_ref[m], g, nt, preferred_element_type=F32)
    lstat, rstat = lstat_ref[...], rstat_ref[...]
    new_left = (BETA * lstat.astype(F32) + (1.0 - BETA) * gram_left).astype(BF16)
    left_ref[...] = jnp.where(alive, new_left, lstat)
    cols = parts_ref[:, :, pl.ds(pl.multiple_of(lax.div(m, 2) * 128, 128), 128)].reshape(width, 128)
    gram_ref[...] = lax.dot_general(cols, g, tn, preferred_element_type=F32)
    gram_right = gram_ref[pl.ds(pl.multiple_of(lax.rem(m, 2) * rows, rows), rows), :]
    new_right = (BETA * rstat.astype(F32) + (1.0 - BETA) * gram_right).astype(BF16)
    right_ref[...] = jnp.where(alive, new_right, rstat)
    blocks = [(ref.at[k], back) for ref, backs in zip(root_refs, BACK) for k, back in enumerate(backs)]
    for i, (ref, back) in enumerate(blocks):
        lroot_ref[pl.ds(i * rows, rows), :] = ref[0]
        place = lax.rem(m + n_mp - back, n_mp) * rows
        rroot_ref[pl.ds(pl.multiple_of(place, rows), rows), :] = ref[1]
    middle = lax.dot_general(g, rroot_ref[...], nt, preferred_element_type=F32).astype(BF16)
    pre = jnp.dot(lroot_ref[...], middle, preferred_element_type=F32)
    g_float = g.astype(F32)
    squares = jnp.sum(g_float * g_float)
    pre_squares = jnp.sum(pre * pre)
    top = jnp.full((1, 1), squares, F32) / cells
    bottom = jnp.full((1, 1), pre_squares, F32) / cells + EPS
    scale = jnp.sqrt(top) / jnp.sqrt(bottom)
    new_update = (-RATE * scale * pre[:rows]).astype(BF16)
    update_ref[...] = jnp.where(alive, new_update, jnp.zeros_like(new_update))


VMEM = pl.BlockSpec(memory_space=pltpu.VMEM)
SMEM = pl.BlockSpec(memory_space=pltpu.SMEM)
LIMIT = pltpu.CompilerParams(vmem_limit_bytes=16 * 1024 * 1024)


def kernel_call(kernel, out_shape, scratch, scalars, *arrays):
    return pl.pallas_call(
        kernel,
        out_shape=out_shape,
        in_specs=[SMEM] * len(scalars) + [VMEM] * len(arrays),
        out_specs=jax.tree.map(lambda _: VMEM, out_shape),
        scratch_shapes=scratch,
        compiler_params=LIMIT,
    )(*scalars, *arrays)


def bf16(*shape):
    return jax.ShapeDtypeStruct(shape, BF16)


def on_device(grads, slot_blocks, counts, left_stat, right_stat, left_root, right_root):
    terms = grads[0]
    nblk, rows, width = terms.shape
    n_mp = width // rows
    core = lax.axis_index("c")

    half, piece, quarter = rows // NC, rows // (NC * NL), width // NX
    halves = terms.reshape(nblk, NC, half, width)
    away = pl.pallas_call(
        away_kernel,
        out_shape=bf16(nblk, half, width),
        in_specs=[SMEM, pl.BlockSpec(memory_space=pltpu.HBM)],
        out_specs=VMEM,
        scratch_shapes=[pltpu.SemaphoreType.DMA],
        compiler_params=LIMIT,
    )(core.astype(jnp.int32)[None], halves)
    come = lax.ppermute(away, "c", [(0, 1), (1, 0)])

    def shift(a, k):
        return lax.ppermute(a, "mp", [(i, (i + k) % n_mp) for i in range(n_mp)])

    own = jnp.stack([left_root[0, 0], right_root[0, 0].T])[None]
    pairs = pl.pallas_call(
        pair_kernel,
        grid=(nblk // BATCH,),
        out_shape=bf16(NL * NX, nblk, piece, quarter),
        in_specs=[SMEM, VMEM, VMEM],
        out_specs=pl.BlockSpec((NL * NX, BATCH, piece, quarter), lambda i: (0, i, 0, 0)),
        compiler_params=LIMIT,
    )(core.astype(jnp.int32)[None], halves, come)
    along_x = lax.all_to_all(pairs, ("zl", "x"), 0, 0, tiled=True)
    four, one, seven = shift(own, 4), shift(own, 1), shift(own, -1)
    along_x, four, one, seven = lax.optimization_barrier((along_x, four, one, seven))
    owners = slot_blocks.shape[0]
    routed = pl.pallas_call(
        route_kernel,
        grid=(owners // SLOTS,),
        out_shape=bf16(owners, piece, quarter),
        in_specs=[SMEM, VMEM],
        out_specs=pl.BlockSpec((SLOTS, piece, quarter), lambda i: (i, 0, 0)),
        scratch_shapes=[pltpu.VMEM((nblk, piece, quarter), BF16)],
        compiler_params=LIMIT,
    )(slot_blocks[:, 0], along_x)
    live = jnp.stack([counts[0], lax.axis_index("mp").astype(jnp.int32)])
    routed, live = lax.optimization_barrier((routed, live))
    owned = lax.all_to_all(routed, DP, 0, 0, tiled=True)
    up = shift(jnp.concatenate([four, one]), 1)
    down = shift(jnp.concatenate([four, seven]), -1)
    owned, up, down = lax.optimization_barrier((owned, up, down))
    copies = kernel_call(collect_kernel, bf16(n_mp, rows, width), [], (), owned)
    g = lax.all_to_all(copies, "mp", 0, 0, tiled=True)
    roots = (own, four, one, seven, up, down)
    shape = bf16(rows, width)
    outs = kernel_call(
        finish_kernel,
        (shape, shape, shape),
        [pltpu.VMEM((128, width), F32)] + [pltpu.VMEM((width, width), BF16)] * 2,
        (live,),
        g,
        left_stat[0, 0],
        right_stat[0, 0],
        *roots,
    )
    return tuple(o[None, None] for o in outs)


def solution(mesh):
    fine = Mesh(mesh.devices.reshape(NH, NL, NX, NC, mesh.devices.shape[1]), (*DP, "mp"))
    rows = P(DP, None, "mp", None)
    return jax.shard_map(
        on_device,
        mesh=fine,
        in_specs=(rows, P(), P(DP), rows, rows, rows, P(DP, None, None, "mp")),
        out_specs=(rows, rows, rows),
        check_vma=False,
    )
```
